32 devices in a mesh: rve: 2 (over x), gx: 16 (over z, y, core).
Axes of the slice: x: 2, y: 2, z: 4, core: 2. Of those that a mesh axis runs over, the one named last changes fastest.
Arguments:
- tokens: bfloat16 [32, 16, 128, 128], P(('rve', 'gx')), parts along dimension 0, may hold values from -16 to 16
- cotangent: bfloat16 [32, 16, 128, 128], P(('rve', 'gx')), parts along dimension 0, may hold values from -6 to 6
- offsets: int32 [3], replicated, may hold values from 1 to 7
- norm_gain: float32 [128], replicated, may hold values from 0.5 to 1.5
- qkv_weight: bfloat16 [128, 384], replicated, may hold values from -2.5 to 2.5
- proj_weight: bfloat16 [128, 128], replicated, may hold values from -0.5 to 0.5
Outputs:
- grad_tokens: bfloat16 [32, 16, 128, 128], P(('rve', 'gx')), parts along dimension 0
- grad_qkv: float32 [256, 384], P('rve'), parts along dimension 0
- grad_proj: float32 [256, 128], P('rve'), parts along dimension 0
- grad_gain: float32 [256], P('rve'), parts along dimension 0
The draws below stay inside these ranges and needn't reach their ends.
There are 2 independent parts, one for each index of `rve`. The reference program is written for one: setup_inputs(seed, part) draws one part's arguments, and reference() takes and returns one part's arrays. A program takes and returns all parts, laid end to end along the dimension named above; an argument that names none is the same for every part. Nothing has to cross between parts.
All inputs are finite; a program needn't handle non-finite values.
Results may differ from the reference program's by a relative error of at most 0.012.
The reference program's roundings to bfloat16 on the way count: a program that leaves them out, or rounds other values in their place, can miss the bound.
Values may be sent and summed in bfloat16 or wider, within the bound.
A program may use at most 64 MiB of HBM per device.

```python
import jax
import jax.numpy as jnp
from jax import lax

C = 128
H = 4
G2 = 16
G3 = 128
NX = 16
TOKENS = 32768


def draw_tokens(key, part):
    values = jax.random.normal(key, (NX, G2, G3, C), jnp.float32)
    return jnp.clip(values, -16.0, 16.0).astype(jnp.bfloat16)


def draw_qkv_weight(key, part):
    base_key = jax.random.fold_in(key, 0)
    matrix = jax.random.normal(base_key, (C, 3 * C), jnp.float32) * C ** (-0.5)
    return jnp.clip(matrix, -2.5, 2.5).astype(jnp.bfloat16)


def level_of(key, extent, shards, smallest, high):
    factor_of = 1.0
    for axis_at, blocks in shards:
        draws = jax.random.uniform(jax.random.fold_in(jax.random.fold_in(key, 6), axis_at), (blocks,), jnp.float32, smallest / len(shards), high / len(shards))
        factor_of = factor_of * jnp.repeat(jnp.exp(draws), extent[axis_at] // blocks).reshape((-1,) + (1,) * (len(extent) - 1 - axis_at))
    return factor_of


def normal_values(rng, dims, width, limit, cuts=(), held_as=jnp.bfloat16):
    array = jax.random.normal(rng, dims, jnp.float32) * width
    if len(cuts) > 0:
        array = level_of(rng, dims, cuts, -0.22, 0.18) * array
    return jnp.clip(array, min=-limit, max=limit).astype(held_as)


def setup_inputs(seed: int = 0, part: int = 0) -> dict:
    keys = jax.random.split(jax.random.key(seed), 7)
    part_keys = jax.random.split(jax.random.fold_in(keys[6], part), 7)
    tokens = draw_tokens(jax.random.fold_in(jax.random.fold_in(keys[6], part), 71), part)
    cotangent = normal_values(part_keys[1], (NX, G2, G3, C), 1.0, 6.0, ((0, 16),))
    offsets = jax.random.randint(keys[2], (3,), 1, 8).astype(jnp.int32)
    norm_gain = jnp.clip(1.0 + 0.1 * jax.random.normal(keys[3], (C,), jnp.float32), 0.5, 1.5)
    qkv_weight = draw_qkv_weight(jax.random.fold_in(keys[6], 71), part)
    proj_weight = normal_values(keys[5], (C, C), C ** -0.5, 0.5)
    return {"tokens": tokens, "cotangent": cotangent, "offsets": offsets, "norm_gain": norm_gain, "qkv_weight": qkv_weight, "proj_weight": proj_weight}


epsilon = 1e-05

def layer_norm(inputs, norm_gain):
    values = inputs.astype(jnp.float32)
    centre = values - lax.optimization_barrier(jnp.mean(values, -1, keepdims=True))
    inv_std = lax.rsqrt(lax.optimization_barrier(jnp.mean(centre * centre, -1, keepdims=True)) + epsilon)
    scaled = centre * inv_std
    return ((scaled * norm_gain).astype(jnp.bfloat16), scaled, inv_std)

def layer_norm_back(grad_norm, scaled, inv_std, norm_gain):
    grad_hat = grad_norm * norm_gain
    return inv_std * (grad_hat - lax.optimization_barrier(jnp.mean(grad_hat, -1, keepdims=True)) - scaled * lax.optimization_barrier(jnp.mean(grad_hat * scaled, -1, keepdims=True)))

def attend_back(queries, keyval, grad_out, head_count):
    query_rows, features = queries.shape
    key_rows = keyval.shape[0]
    head_dim = features // head_count
    factor = head_dim ** (-0.5)
    query_heads = queries.astype(jnp.float32).reshape(query_rows, head_count, head_dim)
    key_heads = keyval[:, :features].astype(jnp.float32).reshape(key_rows, head_count, head_dim)
    value_heads = keyval[:, features:].astype(jnp.float32).reshape(key_rows, head_count, head_dim)
    grad_heads = grad_out.astype(jnp.float32).reshape(query_rows, head_count, head_dim)
    scores = jnp.einsum('qhd,khd->hqk', query_heads, key_heads) * factor
    exponent = jnp.exp(scores - lax.optimization_barrier(jnp.max(scores, -1, keepdims=True)))
    prob_weights = exponent / lax.optimization_barrier(jnp.sum(exponent, -1, keepdims=True))
    prob_bf = prob_weights.astype(jnp.bfloat16)
    prob_cast = prob_bf.astype(jnp.float32)
    attended = jnp.einsum('hqk,khd->qhd', prob_cast, value_heads).astype(jnp.bfloat16).reshape(query_rows, features)
    grad_value = jnp.einsum('hqk,qhd->khd', prob_cast, grad_heads)
    grad_prob = jnp.einsum('qhd,khd->hqk', grad_heads, value_heads)
    grad_score = (prob_weights * (grad_prob - lax.optimization_barrier(jnp.sum(prob_weights * grad_prob, -1, keepdims=True))) * factor).astype(jnp.bfloat16)
    score_cast = grad_score.astype(jnp.float32)
    grad_query = jnp.einsum('hqk,khd->qhd', score_cast, key_heads).astype(jnp.bfloat16).reshape(query_rows, features)
    grad_key = jnp.einsum('hqk,qhd->khd', score_cast, query_heads)
    grad_kv = jnp.concatenate([grad_key.reshape(key_rows, features), grad_value.reshape(key_rows, features)], -1)
    return (attended, grad_query, grad_kv)

def reference(tokens, cotangent, offsets, norm_gain, qkv_weight, proj_weight):
    features = tokens.shape[-1]
    shifted_tokens = tokens
    shifted_cotangent = cotangent
    for axis_pos in range(3):
        shifted_tokens = jnp.roll(shifted_tokens, -offsets[axis_pos], axis=axis_pos)
        shifted_cotangent = jnp.roll(shifted_cotangent, -offsets[axis_pos], axis=axis_pos)

    def to_windows(grid_field):
        blocked = grid_field.reshape(NX // 8, 8, G2 // 8, 8, G3 // 8, 8, features)
        return blocked.transpose(0, 2, 4, 1, 3, 5, 6).reshape(-1, 512, features)

    def from_windows(windows):
        blocked = windows.reshape(NX // 8, G2 // 8, G3 // 8, 8, 8, 8, features)
        return blocked.transpose(0, 3, 1, 4, 2, 5, 6).reshape(NX, G2, G3, features)
    kv_trans = qkv_weight[:, features:].astype(jnp.float32).T
    query_trans = qkv_weight[:, :features].T

    def window_step(totals, blocks):
        acc_qkv, acc_proj, acc_gain = totals
        window_tok, window_cot = blocks
        normed, scaled, inv_std = layer_norm(window_tok, norm_gain)
        projected = jnp.dot(normed, qkv_weight, preferred_element_type=jnp.float32).astype(jnp.bfloat16)
        grad_out = jnp.dot(window_cot, proj_weight.T, preferred_element_type=jnp.float32).astype(jnp.bfloat16)
        attended, grad_query, grad_kv = attend_back(projected[:, :features], projected[:, features:], grad_out, H)
        acc_proj = acc_proj + jnp.dot(attended.T, window_cot, preferred_element_type=jnp.float32)
        grad_norm = jnp.dot(grad_query, query_trans, preferred_element_type=jnp.float32) + jnp.dot(grad_kv, kv_trans, precision=lax.Precision.HIGHEST)
        grad_q_w = jnp.dot(normed.T, grad_query, preferred_element_type=jnp.float32)
        grad_kv_w = jnp.dot(normed.astype(jnp.float32).T, grad_kv, precision=lax.Precision.HIGHEST)
        acc_qkv = acc_qkv + jnp.concatenate([grad_q_w, grad_kv_w], 1)
        acc_gain = acc_gain + lax.optimization_barrier(jnp.sum(grad_norm * scaled, 0))
        grad_window = (window_cot.astype(jnp.float32) + layer_norm_back(grad_norm, scaled, inv_std, norm_gain)).astype(jnp.bfloat16)
        return ((acc_qkv, acc_proj, acc_gain), grad_window)
    initial = (jnp.zeros((features, 3 * features), jnp.float32), jnp.zeros((features, features), jnp.float32), jnp.zeros((features,), jnp.float32))
    totals, grad_windows = lax.scan(window_step, initial, (to_windows(shifted_tokens), to_windows(shifted_cotangent)))
    grad_tokens = from_windows(grad_windows)
    for axis_pos in range(3):
        grad_tokens = jnp.roll(grad_tokens, offsets[axis_pos], axis=axis_pos)
    norm_scale = TOKENS ** (-0.5)
    return (grad_tokens, totals[0] * norm_scale, totals[1] * norm_scale, totals[2] * norm_scale)
```

```python
import jax
import jax.numpy as jnp
from jax import lax
from jax.experimental import pallas as pl
from jax.experimental.pallas import tpu as pltpu
from jax.sharding import PartitionSpec as P

H = 4
W = 8
EPSILON = 1e-05
F32 = jnp.float32
BF16 = jnp.bfloat16


def nn(a, b):
    return lax.dot_general(a, b, (((1,), (0,)), ((), ())), preferred_element_type=F32)


def nt(a, b):
    return lax.dot_general(a, b, (((1,), (1,)), ((), ())), preferred_element_type=F32)


def split_two(value):
    high = value.astype(BF16)
    low = (value - high.astype(F32)).astype(BF16)
    return high, low


def window_kernel(
    offsets_ref, data_ref, gain_ref, qkv_ref, back_ref, proj_t_ref, mask_ref,
    grad_ref, acc_qkv_ref, acc_proj_ref, acc_gain_ref,
    tok_ref, cot_ref, res_ref,
):
    extent_x, _, extent_y = data_ref.shape[:3]
    features = data_ref.shape[-1]
    step = pl.program_id(0)
    per_y = extent_y // W
    first_x = (step // per_y) * W + offsets_ref[0]
    first_y = (step % per_y) * W + offsets_ref[1]

    def place(i, j):
        return lax.rem(first_x + i, extent_x), lax.rem(first_y + j, extent_y)

    for i in range(W):
        for j in range(W):
            at_x, at_y = place(i, j)
            rows = pl.ds((i * W + j) * W, W)
            tok_ref[rows, :] = data_ref[at_x, 0, at_y].astype(F32)
            cot_ref[rows, :] = data_ref[at_x, 1, at_y].astype(F32)

    gain = gain_ref[...]
    values = tok_ref[...]
    centre = values - jnp.mean(values, -1, keepdims=True)
    inv_std = lax.rsqrt(jnp.mean(centre * centre, -1, keepdims=True) + EPSILON)
    scaled = centre * inv_std
    normed = (scaled * gain).astype(BF16)
    cot = cot_ref[...].astype(BF16)
    projected = nn(normed, qkv_ref[...]).astype(BF16)
    queries = projected[:, :features]
    keys = projected[:, features : 2 * features]
    values_bf = projected[:, 2 * features :]
    grad_out = nn(cot, proj_t_ref[...]).astype(BF16)
    keys_t = keys.T
    values_t = values_bf.T

    head_dim = features // H
    factor = head_dim ** (-0.5)
    exp_factor = factor * 1.4426950408889634
    grad_key = jnp.zeros((W * W * W, features), F32)
    grad_value = jnp.zeros((W * W * W, features), F32)
    attended_rows = []
    grad_query_rows = []
    for head in range(H):
        mask = mask_ref[head : head + 1, :]
        head_rows = slice(head * head_dim, (head + 1) * head_dim)
        query_h = queries * mask
        grad_h = grad_out * mask
        scores = nt(keys, query_h)
        exponent = jnp.exp2((scores - jnp.max(scores, 0, keepdims=True)) * exp_factor)
        prob = exponent * (1.0 / jnp.sum(exponent, 0, keepdims=True))
        prob_bf = prob.astype(BF16)
        attended_rows.append(nn(values_t[head_rows], prob_bf).astype(BF16))
        grad_value = grad_value + nn(prob_bf, grad_h)
        grad_prob = nt(values_bf, grad_h)
        row_sum = jnp.sum(prob * grad_prob, 0, keepdims=True)
        grad_score = (prob * (grad_prob - row_sum) * factor).astype(BF16)
        grad_query_rows.append(nn(keys_t[head_rows], grad_score).astype(BF16))
        grad_key = grad_key + nn(grad_score, query_h)

    attended_t = jnp.concatenate(attended_rows, 0)
    grad_query = jnp.concatenate(grad_query_rows, 0).T
    key_high, key_low = split_two(grad_key)
    value_high, value_low = split_two(grad_value)
    terms = jnp.concatenate([grad_query, key_high, value_high, key_low, value_low], 1)
    grad_norm = nn(terms, back_ref[...])
    weight_terms = nn(normed.T, terms)
    add_qkv = weight_terms[:, : 3 * features] + jnp.concatenate(
        [jnp.zeros((features, features), F32), weight_terms[:, 3 * features :]], 1
    )
    add_proj = nn(attended_t, cot)
    add_gain = jnp.sum(grad_norm * scaled, 0, keepdims=True)

    @pl.when(step == 0)
    def _():
        acc_qkv_ref[...] = add_qkv
        acc_proj_ref[...] = add_proj
        acc_gain_ref[...] = add_gain

    @pl.when(step > 0)
    def _():
        acc_qkv_ref[...] += add_qkv
        acc_proj_ref[...] += add_proj
        acc_gain_ref[...] += add_gain

    grad_hat = grad_norm * gain
    res_ref[...] = cot_ref[...] + inv_std * (
        grad_hat
        - jnp.mean(grad_hat, -1, keepdims=True)
        - scaled * jnp.mean(grad_hat * scaled, -1, keepdims=True)
    )
    for i in range(W):
        for j in range(W):
            at_x, at_y = place(i, j)
            grad_ref[at_x, at_y] = res_ref[pl.ds((i * W + j) * W, W), :].astype(BF16)


def windows_back(offsets, data, norm_gain, qkv_weight, proj_weight):
    extent_x, _, extent_y, _, features = data.shape
    steps = (extent_x // W) * (extent_y // W)
    weight_t = qkv_weight.T
    back = jnp.concatenate([weight_t, weight_t[features:]], 0)
    lanes = jnp.arange(features) // (features // H)
    mask = (lanes[None, :] == jnp.arange(H)[:, None]).astype(BF16)
    whole = pl.BlockSpec(memory_space=pltpu.VMEM)
    rows = W * W * W
    return pl.pallas_call(
        window_kernel,
        grid=(steps,),
        in_specs=[pl.BlockSpec(memory_space=pltpu.SMEM)] + [whole] * 6,
        out_specs=[whole] * 4,
        out_shape=[
            jax.ShapeDtypeStruct((extent_x, extent_y, W, features), BF16),
            jax.ShapeDtypeStruct((features, 3 * features), F32),
            jax.ShapeDtypeStruct((features, features), F32),
            jax.ShapeDtypeStruct((1, features), F32),
        ],
        scratch_shapes=[pltpu.VMEM((rows, features), F32)] * 3,
        compiler_params=pltpu.CompilerParams(vmem_limit_bytes=48 * 1024 * 1024),
        cost_estimate=pl.CostEstimate(
            flops=steps * 12 * rows * rows * features,
            bytes_accessed=3 * data.size,
            transcendentals=steps * H * rows * rows,
        ),
    )(offsets, data, norm_gain.reshape(1, -1), qkv_weight, back, proj_weight.T, mask)


def shift_rows(field, offset, sign):
    count = lax.axis_size("gx")
    for bit_pos in range(3):
        by = sign * (1 << bit_pos)
        moved = lax.ppermute(field, "gx", [(i, (i + by) % count) for i in range(count)])
        field = jnp.where(offset >> bit_pos & 1 == 1, moved, field)
    return field


def exchange(pieces, group):
    count = lax.axis_size("gx")
    groups = None
    if count != group:
        groups = [list(range(i, i + group)) for i in range(0, count, group)]
    return lax.all_to_all(pieces, "gx", 0, 0, axis_index_groups=groups, tiled=True)


def per_device(tokens, cotangent, offsets, norm_gain, qkv_weight, proj_weight):
    _, extent_y, extent_z, features = tokens.shape
    count = lax.axis_size("gx")
    group = extent_z // W
    offset_x = offsets[0]
    stacked = jnp.concatenate([tokens, cotangent], 0)
    if count != group:
        stacked = shift_rows(stacked, offset_x, -1)
        offsets = offsets * jnp.array([0, 1, 1], offsets.dtype)
    stacked = jnp.roll(stacked, -offsets[2], axis=2)
    pieces = stacked.reshape(2, extent_y, group, W, features).transpose(2, 0, 1, 3, 4)
    data = exchange(pieces, group)
    grads, acc_qkv, acc_proj, acc_gain = windows_back(
        offsets, data, norm_gain, qkv_weight, proj_weight
    )
    back = exchange(grads, group)
    field = back.transpose(1, 0, 2, 3).reshape(1, extent_y, extent_z, features)
    field = jnp.roll(field, offsets[2], axis=2)
    if count != group:
        field = shift_rows(field, offset_x, 1)
    summed = lax.psum((acc_qkv, acc_proj, acc_gain[0]), "gx")
    norm_scale = (count * extent_y * extent_z) ** (-0.5)
    return (field, summed[0] * norm_scale, summed[1] * norm_scale, summed[2] * norm_scale)


def solution(mesh):
    rows = P(("rve", "gx"), None, None, None)
    return jax.shard_map(
        per_device,
        mesh=mesh,
        in_specs=(rows, rows, P(), P(), P(), P()),
        out_specs=(rows, P("rve", None), P("rve", None), P("rve")),
        check_vma=False,
    )
```

```python
import jax
import jax.numpy as jnp
from jax import lax
from jax.experimental import pallas as pl
from jax.experimental.pallas import tpu as pltpu
from jax.sharding import PartitionSpec as P

H = 4
W = 8
EPSILON = 1e-05
F32 = jnp.float32
BF16 = jnp.bfloat16


def nn(a, b):
    return lax.dot_general(a, b, (((1,), (0,)), ((), ())), preferred_element_type=F32)


def nt(a, b):
    return lax.dot_general(a, b, (((1,), (1,)), ((), ())), preferred_element_type=F32)


def split_two(value):
    high = value.astype(BF16)
    low = (value - high.astype(F32)).astype(BF16)
    return high, low


def window_kernel(
    offsets_ref, data_ref, gain_ref, qkv_ref, back_ref, proj_t_ref, mask_ref,
    grad_ref, acc_ref,
    tok_ref, cot_ref, res_ref,
):
    extent_x, _, extent_y = data_ref.shape[:3]
    features = data_ref.shape[-1]
    step = pl.program_id(0)
    per_y = extent_y // W
    first_x = (step // per_y) * W + offsets_ref[0]
    first_y = (step % per_y) * W + offsets_ref[1]

    def place(i, j):
        return lax.rem(first_x + i, extent_x), lax.rem(first_y + j, extent_y)

    for i in range(W):
        for j in range(W):
            at_x, at_y = place(i, j)
            rows = pl.ds((i * W + j) * W, W)
            tok_ref[rows, :] = data_ref[at_x, 0, at_y].astype(F32)
            cot_ref[rows, :] = data_ref[at_x, 1, at_y].astype(F32)

    gain = gain_ref[...]
    values = tok_ref[...]
    centre = values - jnp.mean(values, -1, keepdims=True)
    inv_std = lax.rsqrt(jnp.mean(centre * centre, -1, keepdims=True) + EPSILON)
    scaled = centre * inv_std
    normed = (scaled * gain).astype(BF16)
    cot = cot_ref[...].astype(BF16)
    projected = nn(normed, qkv_ref[...]).astype(BF16)
    queries = projected[:, :features]
    keys = projected[:, features : 2 * features]
    values_bf = projected[:, 2 * features :]
    grad_out = nn(cot, proj_t_ref[...]).astype(BF16)
    keys_t = keys.T
    values_t = values_bf.T

    head_dim = features // H
    factor = head_dim ** (-0.5)
    exp_factor = factor * 1.4426950408889634
    grad_key = jnp.zeros((W * W * W, features), F32)
    grad_value = jnp.zeros((W * W * W, features), F32)
    attended_rows = []
    grad_query_rows = []
    for head in range(H):
        mask = mask_ref[head : head + 1, :]
        head_rows = slice(head * head_dim, (head + 1) * head_dim)
        query_h = queries * mask
        grad_h = grad_out * mask
        scores = nt(keys, query_h)
        exponent = jnp.exp2((scores - jnp.max(scores, 0, keepdims=True)) * exp_factor)
        prob = exponent * (1.0 / jnp.sum(exponent, 0, keepdims=True))
        prob_bf = prob.astype(BF16)
        attended_rows.append(nn(values_t[head_rows], prob_bf).astype(BF16))
        grad_value = grad_value + nn(prob_bf, grad_h)
        grad_prob = nt(values_bf, grad_h)
        row_sum = jnp.sum(prob * grad_prob, 0, keepdims=True)
        grad_score = (prob * (grad_prob - row_sum) * factor).astype(BF16)
        grad_query_rows.append(nn(keys_t[head_rows], grad_score).astype(BF16))
        grad_key = grad_key + nn(grad_score, query_h)

    attended_t = jnp.concatenate(attended_rows, 0)
    grad_query = jnp.concatenate(grad_query_rows, 0).T
    key_high, key_low = split_two(grad_key)
    value_high, value_low = split_two(grad_value)
    terms = jnp.concatenate([grad_query, key_high, value_high, key_low, value_low], 1)
    grad_norm = nn(terms, back_ref[...])
    weight_terms = nn(normed.T, terms)
    add_qkv = weight_terms[:, : 3 * features] + jnp.concatenate(
        [jnp.zeros((features, features), F32), weight_terms[:, 3 * features :]], 1
    )
    add_proj = nn(attended_t, cot)
    add_gain = jnp.sum(grad_norm * scaled, 0, keepdims=True)

    @pl.when(step == 0)
    def _():
        acc_ref[...] = jnp.zeros_like(acc_ref)

    acc_ref[:, : 3 * features] += add_qkv
    acc_ref[:, 3 * features : 4 * features] += add_proj
    acc_ref[0:1, 4 * features :] += add_gain

    grad_hat = grad_norm * gain
    res_ref[...] = cot_ref[...] + inv_std * (
        grad_hat
        - jnp.mean(grad_hat, -1, keepdims=True)
        - scaled * jnp.mean(grad_hat * scaled, -1, keepdims=True)
    )
    for i in range(W):
        for j in range(W):
            at_x, at_y = place(i, j)
            grad_ref[at_x, at_y] = res_ref[pl.ds((i * W + j) * W, W), :].astype(BF16)


def windows_back(offsets, data, norm_gain, qkv_weight, proj_weight):
    extent_x, _, extent_y, _, features = data.shape
    steps = (extent_x // W) * (extent_y // W)
    weight_t = qkv_weight.T
    back = jnp.concatenate([weight_t, weight_t[features:]], 0)
    lanes = jnp.arange(features) // (features // H)
    mask = (lanes[None, :] == jnp.arange(H)[:, None]).astype(BF16)
    whole = pl.BlockSpec(memory_space=pltpu.VMEM)
    rows = W * W * W
    return pl.pallas_call(
        window_kernel,
        grid=(steps,),
        in_specs=[pl.BlockSpec(memory_space=pltpu.SMEM)] + [whole] * 6,
        out_specs=[whole] * 2,
        out_shape=[
            jax.ShapeDtypeStruct((extent_x, extent_y, W, features), BF16),
            jax.ShapeDtypeStruct((features, 5 * features), F32),
        ],
        scratch_shapes=[pltpu.VMEM((rows, features), F32)] * 3,
        compiler_params=pltpu.CompilerParams(vmem_limit_bytes=48 * 1024 * 1024),
        cost_estimate=pl.CostEstimate(
            flops=steps * 12 * rows * rows * features,
            bytes_accessed=3 * data.size,
            transcendentals=steps * H * rows * rows,
        ),
    )(offsets, data, norm_gain.reshape(1, -1), qkv_weight, back, proj_weight.T, mask)


def return_kernel(
    group, grads_ref, acc_ref, field_ref, total_ref,
    slots, part, acc_send, acc_recv, all_send, all_recv, grad_send, grad_recv,
):
    me = lax.axis_index("gx")
    mine = lax.rem(me, group)
    base = me - mine
    others = [lax.rem(mine + r, group) for r in range(1, group)]

    barrier = pltpu.get_barrier_semaphore()
    for other in others:
        pl.semaphore_signal(
            barrier, inc=1, device_id={"gx": base + other}, device_id_type=pl.DeviceIdType.MESH
        )
    pl.semaphore_wait(barrier, group - 1)

    def copies(source, target, send, recv):
        out = []
        for at, other in enumerate(others):
            copy = pltpu.make_async_remote_copy(
                src_ref=source(other),
                dst_ref=target(at),
                send_sem=send.at[at],
                recv_sem=recv.at[at],
                device_id={"gx": base + other},
                device_id_type=pl.DeviceIdType.MESH,
            )
            copy.start()
            out.append(copy)
        return out

    terms = copies(lambda p: acc_ref.at[p], lambda at: slots.at[at], acc_send, acc_recv)
    rows = copies(lambda p: grads_ref.at[p], lambda at: field_ref.at[mine], grad_send, grad_recv)
    field_ref[mine] = grads_ref[mine]
    summed = acc_ref[mine]
    for at, copy in enumerate(terms):
        copy.wait_recv()
        summed = summed + slots[at]
    part[...] = summed
    sums = copies(lambda p: part, lambda at: total_ref.at[mine], all_send, all_recv)
    total_ref[mine] = summed
    for copy in rows + sums:
        copy.wait_recv()
    for copy in terms + rows + sums:
        copy.wait_send()


def return_and_sum(grads, acc, group):
    features = grads.shape[-1]
    pieces = grads.reshape(group, -1, features)
    parts = acc.reshape(group, -1, acc.shape[-1])
    whole = pl.BlockSpec(memory_space=pltpu.VMEM)
    sems = pltpu.SemaphoreType.DMA((group - 1,))
    field, total = pl.pallas_call(
        lambda *refs: return_kernel(group, *refs),
        in_specs=[whole] * 2,
        out_specs=[whole] * 2,
        out_shape=[
            jax.ShapeDtypeStruct(pieces.shape, pieces.dtype),
            jax.ShapeDtypeStruct(parts.shape, parts.dtype),
        ],
        scratch_shapes=[
            pltpu.VMEM((group - 1,) + parts.shape[1:], F32),
            pltpu.VMEM(parts.shape[1:], F32),
        ]
        + [sems] * 6,
        compiler_params=pltpu.CompilerParams(
            collective_id=0, has_side_effects=True, vmem_limit_bytes=32 * 1024 * 1024
        ),
        name="return_and_sum",
    )(pieces, parts)
    return field.reshape(grads.shape), total.reshape(acc.shape)


def shift_rows(field, offset, sign):
    count = lax.axis_size("gx")
    for bit_pos in range(3):
        by = sign * (1 << bit_pos)
        moved = lax.ppermute(field, "gx", [(i, (i + by) % count) for i in range(count)])
        field = jnp.where(offset >> bit_pos & 1 == 1, moved, field)
    return field


def exchange(pieces, group):
    count = lax.axis_size("gx")
    groups = None
    if count != group:
        groups = [list(range(i, i + group)) for i in range(0, count, group)]
    return lax.all_to_all(pieces, "gx", 0, 0, axis_index_groups=groups, tiled=True)


def per_device(tokens, cotangent, offsets, norm_gain, qkv_weight, proj_weight):
    _, extent_y, extent_z, features = tokens.shape
    count = lax.axis_size("gx")
    group = extent_z // W
    offset_x = offsets[0]
    stacked = jnp.concatenate([tokens, cotangent], 0)
    if count != group:
        stacked = shift_rows(stacked, offset_x, -1)
        offsets = offsets * jnp.array([0, 1, 1], offsets.dtype)
    stacked = jnp.roll(stacked, -offsets[2], axis=2)
    pieces = stacked.reshape(2, extent_y, group, W, features).transpose(2, 0, 1, 3, 4)
    data = exchange(pieces, group)
    grads, acc = windows_back(offsets, data, norm_gain, qkv_weight, proj_weight)
    back, total = return_and_sum(grads, acc, group)
    field = back.transpose(1, 0, 2, 3).reshape(1, extent_y, extent_z, features)
    field = jnp.roll(field, offsets[2], axis=2)
    if count != group:
        field = shift_rows(field, offset_x, 1)
        total = lax.psum(total * (1.0 / group), "gx")
    total = total * (count * extent_y * extent_z) ** (-0.5)
    return (
        field,
        total[:, : 3 * features],
        total[:, 3 * features : 4 * features],
        total[0, 4 * features :],
    )


def solution(mesh):
    rows = P(("rve", "gx"), None, None, None)
    return jax.shard_map(
        per_device,
        mesh=mesh,
        in_specs=(rows, rows, P(), P(), P(), P()),
        out_specs=(rows, P("rve", None), P("rve", None), P("rve")),
        check_vma=False,
    )
```

```python
import jax
import jax.numpy as jnp
from jax import lax
from jax.experimental import pallas as pl
from jax.experimental.pallas import tpu as pltpu
from jax.sharding import PartitionSpec as P

H = 4
W = 8
EPSILON = 1e-05
F32 = jnp.float32
BF16 = jnp.bfloat16


def nn(a, b):
    return lax.dot_general(a, b, (((1,), (0,)), ((), ())), preferred_element_type=F32)


def nt(a, b):
    return lax.dot_general(a, b, (((1,), (1,)), ((), ())), preferred_element_type=F32)


def split_two(value):
    high = value.astype(BF16)
    low = (value - high.astype(F32)).astype(BF16)
    return high, low


def window_kernel(
    offsets_ref, data_ref, gain_ref, qkv_ref, back_ref, proj_t_ref, mask_ref, start_ref,
    grad_ref, acc_ref,
    tok_ref, cot_ref, res_ref,
):
    extent_x, _, extent_y = data_ref.shape[:3]
    features = data_ref.shape[-1]
    step = pl.program_id(0)
    per_y = extent_y // W
    first_x = (step // per_y) * W + offsets_ref[0]
    first_y = (step % per_y) * W

    def place(i, j):
        return lax.rem(first_x + i, extent_x), first_y + j

    for i in range(W):
        for j in range(W):
            at_x, at_y = place(i, j)
            rows = pl.ds((i * W + j) * W, W)
            tok_ref[rows, :] = data_ref[at_x, 0, at_y].astype(F32)
            cot_ref[rows, :] = data_ref[at_x, 1, at_y].astype(F32)

    gain = gain_ref[...]
    values = tok_ref[...]
    centre = values - jnp.mean(values, -1, keepdims=True)
    inv_std = lax.rsqrt(jnp.mean(centre * centre, -1, keepdims=True) + EPSILON)
    scaled = centre * inv_std
    normed = (scaled * gain).astype(BF16)
    cot = cot_ref[...].astype(BF16)
    projected = nn(normed, qkv_ref[...]).astype(BF16)
    queries = projected[:, :features]
    keys = projected[:, features : 2 * features]
    values_bf = projected[:, 2 * features :]
    grad_out = nn(cot, proj_t_ref[...]).astype(BF16)
    keys_t = keys.T
    values_t = values_bf.T

    head_dim = features // H
    factor = head_dim ** (-0.5)
    exp_factor = factor * 1.4426950408889634
    grad_key = jnp.zeros((W * W * W, features), F32)
    grad_value = jnp.zeros((W * W * W, features), F32)
    attended_rows = []
    grad_query_rows = []
    for head in range(H):
        mask = mask_ref[head : head + 1, :]
        head_rows = slice(head * head_dim, (head + 1) * head_dim)
        query_h = queries * mask
        grad_h = grad_out * mask
        scores = nt(keys, query_h)
        exponent = jnp.exp2((scores - jnp.max(scores, 0, keepdims=True)) * exp_factor)
        prob = exponent * (1.0 / jnp.sum(exponent, 0, keepdims=True))
        prob_bf = prob.astype(BF16)
        attended_rows.append(nn(values_t[head_rows], prob_bf).astype(BF16))
        grad_value = grad_value + nn(prob_bf, grad_h)
        grad_prob = nt(values_bf, grad_h)
        row_sum = jnp.sum(prob * grad_prob, 0, keepdims=True)
        grad_score = (prob * (grad_prob - row_sum) * factor).astype(BF16)
        grad_query_rows.append(nn(keys_t[head_rows], grad_score).astype(BF16))
        grad_key = grad_key + nn(grad_score, query_h)

    attended_t = jnp.concatenate(attended_rows, 0)
    grad_query = jnp.concatenate(grad_query_rows, 0).T
    key_high, key_low = split_two(grad_key)
    value_high, value_low = split_two(grad_value)
    terms = jnp.concatenate([grad_query, key_high, value_high, key_low, value_low], 1)
    grad_norm = nn(terms, back_ref[...])
    weight_terms = nn(normed.T, terms)
    add_qkv = weight_terms[:, : 3 * features] + jnp.concatenate(
        [jnp.zeros((features, features), F32), weight_terms[:, 3 * features :]], 1
    )
    add_proj = nn(attended_t, cot)
    add_gain = jnp.sum(grad_norm * scaled, 0, keepdims=True)

    @pl.when(step == 0)
    def _():
        acc_ref[...] = start_ref[...]

    acc_ref[:, : 3 * features] += add_qkv
    acc_ref[:, 3 * features : 4 * features] += add_proj
    acc_ref[0:1, 4 * features :] += add_gain

    grad_hat = grad_norm * gain
    res_ref[...] = cot_ref[...] + inv_std * (
        grad_hat
        - jnp.mean(grad_hat, -1, keepdims=True)
        - scaled * jnp.mean(grad_hat * scaled, -1, keepdims=True)
    )
    for i in range(W):
        for j in range(W):
            at_x, at_y = place(i, j)
            grad_ref[at_x, at_y] = res_ref[pl.ds((i * W + j) * W, W), :].astype(BF16)


def windows_back(offsets, data, norm_gain, qkv_weight, proj_weight, start):
    extent_x, _, extent_y, _, features = data.shape
    steps = (extent_x // W) * (extent_y // W)
    weight_t = qkv_weight.T
    back = jnp.concatenate([weight_t, weight_t[features:]], 0)
    lanes = jnp.arange(features) // (features // H)
    mask = (lanes[None, :] == jnp.arange(H)[:, None]).astype(BF16)
    whole = pl.BlockSpec(memory_space=pltpu.VMEM)
    rows = W * W * W
    return pl.pallas_call(
        window_kernel,
        grid=(steps,),
        in_specs=[pl.BlockSpec(memory_space=pltpu.SMEM)] + [whole] * 7,
        out_specs=[whole] * 2,
        out_shape=[
            jax.ShapeDtypeStruct((extent_x, extent_y, W, features), BF16),
            jax.ShapeDtypeStruct((features, 5 * features), F32),
        ],
        scratch_shapes=[pltpu.VMEM((rows, features), F32)] * 3,
        compiler_params=pltpu.CompilerParams(vmem_limit_bytes=48 * 1024 * 1024),
        cost_estimate=pl.CostEstimate(
            flops=steps * 12 * rows * rows * features,
            bytes_accessed=3 * data.size,
            transcendentals=steps * H * rows * rows,
        ),
    )(offsets, data, norm_gain.reshape(1, -1), qkv_weight, back, proj_weight.T, mask, start)


def return_kernel(
    group, grads_ref, acc_ref, field_ref, total_ref,
    slots, part, acc_send, acc_recv, all_send, all_recv, grad_send, grad_recv,
):
    me = lax.axis_index("gx")
    mine = lax.rem(me, group)
    base = me - mine
    others = [lax.rem(mine + r, group) for r in range(1, group)]

    barrier = pltpu.get_barrier_semaphore()
    for other in others:
        pl.semaphore_signal(
            barrier, inc=1, device_id={"gx": base + other}, device_id_type=pl.DeviceIdType.MESH
        )
    pl.semaphore_wait(barrier, group - 1)

    def copies(source, target, send, recv):
        out = []
        for at, other in enumerate(others):
            copy = pltpu.make_async_remote_copy(
                src_ref=source(other),
                dst_ref=target(at),
                send_sem=send.at[at],
                recv_sem=recv.at[at],
                device_id={"gx": base + other},
                device_id_type=pl.DeviceIdType.MESH,
            )
            copy.start()
            out.append(copy)
        return out

    terms = copies(lambda p: acc_ref.at[p], lambda at: slots.at[at], acc_send, acc_recv)
    rows = copies(lambda p: grads_ref.at[p], lambda at: field_ref.at[mine], grad_send, grad_recv)
    field_ref[mine] = grads_ref[mine]
    summed = acc_ref[mine]
    for at, copy in enumerate(terms):
        copy.wait_recv()
        summed = summed + slots[at]
    part[...] = summed
    sums = copies(lambda p: part, lambda at: total_ref.at[mine], all_send, all_recv)
    total_ref[mine] = summed
    for copy in rows + sums:
        copy.wait_recv()
    for copy in terms + rows + sums:
        copy.wait_send()


def return_and_sum(grads, acc, group):
    features = grads.shape[-1]
    pieces = grads.reshape(group, -1, features)
    parts = acc.reshape(group, -1, acc.shape[-1])
    whole = pl.BlockSpec(memory_space=pltpu.VMEM)
    sems = pltpu.SemaphoreType.DMA((group - 1,))
    field, total = pl.pallas_call(
        lambda *refs: return_kernel(group, *refs),
        in_specs=[whole] * 2,
        out_specs=[whole] * 2,
        out_shape=[
            jax.ShapeDtypeStruct(pieces.shape, pieces.dtype),
            jax.ShapeDtypeStruct(parts.shape, parts.dtype),
        ],
        scratch_shapes=[
            pltpu.VMEM((group - 1,) + parts.shape[1:], F32),
            pltpu.VMEM(parts.shape[1:], F32),
        ]
        + [sems] * 6,
        compiler_params=pltpu.CompilerParams(
            collective_id=0, has_side_effects=True, vmem_limit_bytes=32 * 1024 * 1024
        ),
        name="return_and_sum",
    )(pieces, parts)
    return field.reshape(grads.shape), total.reshape(acc.shape)


def shift_rows(field, offset, sign):
    count = lax.axis_size("gx")
    for bit_pos in range(3):
        by = sign * (1 << bit_pos)
        moved = lax.ppermute(field, "gx", [(i, (i + by) % count) for i in range(count)])
        field = jnp.where(offset >> bit_pos & 1 == 1, moved, field)
    return field


def exchange(pieces, group):
    count = lax.axis_size("gx")
    groups = None
    if count != group:
        groups = [list(range(i, i + group)) for i in range(0, count, group)]
    return lax.all_to_all(pieces, "gx", 0, 0, axis_index_groups=groups, tiled=True)


def per_device(tokens, cotangent, offsets, norm_gain, qkv_weight, proj_weight):
    _, extent_y, extent_z, features = tokens.shape
    count = lax.axis_size("gx")
    group = extent_z // W
    offset_x = offsets[0]
    stacked = jnp.concatenate([tokens, cotangent], 0)
    if count != group:
        stacked = shift_rows(stacked, offset_x, -1)
        offsets = offsets * jnp.array([0, 1, 1], offsets.dtype)
    stacked = jnp.roll(stacked, (-offsets[1], -offsets[2]), axis=(1, 2))
    bands = stacked.reshape(2, extent_y // W, W, group, W, features).transpose(1, 3, 0, 2, 4, 5)
    arrived = [exchange(band, group) for band in bands]
    acc = jnp.zeros((features, 5 * features), F32)
    returned = []
    for at, data in enumerate(arrived):
        grads, acc = windows_back(offsets, data, norm_gain, qkv_weight, proj_weight, acc)
        if at + 1 < len(arrived):
            returned.append(exchange(grads, group))
    back, total = return_and_sum(grads, acc, group)
    returned.append(back)
    field = jnp.concatenate(returned, 1).transpose(1, 0, 2, 3)
    field = field.reshape(1, extent_y, extent_z, features)
    field = jnp.roll(field, (offsets[1], offsets[2]), axis=(1, 2))
    if count != group:
        field = shift_rows(field, offset_x, 1)
        total = lax.psum(total * (1.0 / group), "gx")
    total = total * (count * extent_y * extent_z) ** (-0.5)
    return (
        field,
        total[:, : 3 * features],
        total[:, 3 * features : 4 * features],
        total[0, 4 * features :],
    )


def solution(mesh):
    rows = P(("rve", "gx"), None, None, None)
    return jax.shard_map(
        per_device,
        mesh=mesh,
        in_specs=(rows, rows, P(), P(), P(), P()),
        out_specs=(rows, P("rve", None), P("rve", None), P("rve")),
        check_vma=False,
    )
```

```python
import jax
import jax.numpy as jnp
from jax import lax
from jax.experimental import pallas as pl
from jax.experimental.pallas import tpu as pltpu
from jax.sharding import PartitionSpec as P

H = 4
W = 8
EPSILON = 1e-05
F32 = jnp.float32
BF16 = jnp.bfloat16


def nn(a, b):
    return lax.dot_general(a, b, (((1,), (0,)), ((), ())), preferred_element_type=F32)


def nt(a, b):
    return lax.dot_general(a, b, (((1,), (1,)), ((), ())), preferred_element_type=F32)


def split_two(value):
    high = value.astype(BF16)
    low = (value - high.astype(F32)).astype(BF16)
    return high, low


def window_kernel(
    offsets_ref, data_ref, gain_ref, qkv_ref, back_ref, proj_t_ref, mask_ref,
    grad_ref, acc_ref,
    tok_ref, cot_ref, res_ref,
):
    extent_x, _, extent_y = data_ref.shape[:3]
    features = data_ref.shape[-1]
    step = pl.program_id(0)
    per_y = extent_y // W
    first_x = (step // per_y) * W + offsets_ref[0]
    first_y = (step % per_y) * W + offsets_ref[1]

    def place(i, j):
        return lax.rem(first_x + i, extent_x), lax.rem(first_y + j, extent_y)

    for i in range(W):
        for j in range(W):
            at_x, at_y = place(i, j)
            rows = pl.ds((i * W + j) * W, W)
            tok_ref[rows, :] = data_ref[at_x, 0, at_y].astype(F32)
            cot_ref[rows, :] = data_ref[at_x, 1, at_y].astype(F32)

    gain = gain_ref[...]
    values = tok_ref[...]
    centre = values - jnp.mean(values, -1, keepdims=True)
    inv_std = lax.rsqrt(jnp.mean(centre * centre, -1, keepdims=True) + EPSILON)
    scaled = centre * inv_std
    normed = (scaled * gain).astype(BF16)
    cot = cot_ref[...].astype(BF16)
    projected = nn(normed, qkv_ref[...]).astype(BF16)
    queries = projected[:, :features]
    keys = projected[:, features : 2 * features]
    values_bf = projected[:, 2 * features :]
    grad_out = nn(cot, proj_t_ref[...]).astype(BF16)
    keys_t = keys.T
    values_t = values_bf.T

    head_dim = features // H
    factor = head_dim ** (-0.5)
    exp_factor = factor * 1.4426950408889634
    grad_key = jnp.zeros((W * W * W, features), F32)
    grad_value = jnp.zeros((W * W * W, features), F32)
    attended_rows = []
    grad_query_rows = []
    for head in range(H):
        mask = mask_ref[head : head + 1, :]
        head_rows = slice(head * head_dim, (head + 1) * head_dim)
        query_h = queries * mask
        grad_h = grad_out * mask
        scores = nt(keys, query_h)
        exponent = jnp.exp2((scores - jnp.max(scores, 0, keepdims=True)) * exp_factor)
        prob = exponent * (1.0 / jnp.sum(exponent, 0, keepdims=True))
        prob_bf = prob.astype(BF16)
        attended_rows.append(nn(values_t[head_rows], prob_bf).astype(BF16))
        grad_value = grad_value + nn(prob_bf, grad_h)
        grad_prob = nt(values_bf, grad_h)
        row_sum = jnp.sum(prob * grad_prob, 0, keepdims=True)
        grad_score = (prob * (grad_prob - row_sum) * factor).astype(BF16)
        grad_query_rows.append(nn(keys_t[head_rows], grad_score).astype(BF16))
        grad_key = grad_key + nn(grad_score, query_h)

    attended_t = jnp.concatenate(attended_rows, 0)
    grad_query = jnp.concatenate(grad_query_rows, 0).T
    key_high, key_low = split_two(grad_key)
    value_high, value_low = split_two(grad_value)
    terms = jnp.concatenate([grad_query, key_high, value_high, key_low, value_low], 1)
    grad_norm = nn(terms, back_ref[...])
    weight_terms = nn(normed.T, terms)
    add_qkv = weight_terms[:, : 3 * features] + jnp.concatenate(
        [jnp.zeros((features, features), F32), weight_terms[:, 3 * features :]], 1
    )
    add_proj = nn(attended_t, cot)
    add_gain = jnp.sum(grad_norm * scaled, 0, keepdims=True)

    @pl.when(step == 0)
    def _():
        acc_ref[...] = jnp.zeros_like(acc_ref)

    acc_ref[:, : 3 * features] += add_qkv
    acc_ref[:, 3 * features : 4 * features] += add_proj
    acc_ref[0:1, 4 * features :] += add_gain

    grad_hat = grad_norm * gain
    res_ref[...] = cot_ref[...] + inv_std * (
        grad_hat
        - jnp.mean(grad_hat, -1, keepdims=True)
        - scaled * jnp.mean(grad_hat * scaled, -1, keepdims=True)
    )
    for i in range(W):
        for j in range(W):
            at_x, at_y = place(i, j)
            grad_ref[at_x, at_y] = res_ref[pl.ds((i * W + j) * W, W), :].astype(BF16)


def windows_back(offsets, data, norm_gain, qkv_weight, proj_weight):
    extent_x, _, extent_y, _, features = data.shape
    steps = (extent_x // W) * (extent_y // W)
    weight_t = qkv_weight.T
    back = jnp.concatenate([weight_t, weight_t[features:]], 0)
    lanes = jnp.arange(features) // (features // H)
    mask = (lanes[None, :] == jnp.arange(H)[:, None]).astype(BF16)
    whole = pl.BlockSpec(memory_space=pltpu.VMEM)
    rows = W * W * W
    return pl.pallas_call(
        window_kernel,
        grid=(steps,),
        in_specs=[pl.BlockSpec(memory_space=pltpu.SMEM)] + [whole] * 6,
        out_specs=[whole] * 2,
        out_shape=[
            jax.ShapeDtypeStruct((extent_x, extent_y, W, features), BF16),
            jax.ShapeDtypeStruct((features, 5 * features), F32),
        ],
        scratch_shapes=[pltpu.VMEM((rows, features), F32)] * 3,
        compiler_params=pltpu.CompilerParams(vmem_limit_bytes=48 * 1024 * 1024),
        cost_estimate=pl.CostEstimate(
            flops=steps * 12 * rows * rows * features,
            bytes_accessed=3 * data.size,
            transcendentals=steps * H * rows * rows,
        ),
    )(offsets, data, norm_gain.reshape(1, -1), qkv_weight, back, proj_weight.T, mask)


def return_kernel(
    group, grads_ref, acc_ref, field_ref, total_ref,
    slots, part, acc_send, acc_recv, all_send, all_recv, grad_send, grad_recv,
):
    me = lax.axis_index("gx")
    mine = lax.rem(me, group)
    base = me - mine
    others = [lax.rem(mine + r, group) for r in range(1, group)]

    barrier = pltpu.get_barrier_semaphore()
    for other in others:
        pl.semaphore_signal(
            barrier, inc=1, device_id={"gx": base + other}, device_id_type=pl.DeviceIdType.MESH
        )
    pl.semaphore_wait(barrier, group - 1)

    def copies(source, target, send, recv):
        out = []
        for at, other in enumerate(others):
            copy = pltpu.make_async_remote_copy(
                src_ref=source(other),
                dst_ref=target(at),
                send_sem=send.at[at],
                recv_sem=recv.at[at],
                device_id={"gx": base + other},
                device_id_type=pl.DeviceIdType.MESH,
            )
            copy.start()
            out.append(copy)
        return out

    terms = copies(lambda p: acc_ref.at[p], lambda at: slots.at[at], acc_send, acc_recv)
    rows = copies(lambda p: grads_ref.at[p], lambda at: field_ref.at[mine], grad_send, grad_recv)
    field_ref[mine] = grads_ref[mine]
    summed = acc_ref[mine]
    for at, copy in enumerate(terms):
        copy.wait_recv()
        summed = summed + slots[at]
    part[...] = summed
    sums = copies(lambda p: part, lambda at: total_ref.at[mine], all_send, all_recv)
    total_ref[mine] = summed
    for copy in rows + sums:
        copy.wait_recv()
    for copy in terms + rows + sums:
        copy.wait_send()


def return_and_sum(grads, acc, group):
    features = grads.shape[-1]
    pieces = grads.reshape(group, -1, features)
    parts = acc.reshape(group, -1, acc.shape[-1])
    whole = pl.BlockSpec(memory_space=pltpu.VMEM)
    sems = pltpu.SemaphoreType.DMA((group - 1,))
    field, total = pl.pallas_call(
        lambda *refs: return_kernel(group, *refs),
        in_specs=[whole] * 2,
        out_specs=[whole] * 2,
        out_shape=[
            jax.ShapeDtypeStruct(pieces.shape, pieces.dtype),
            jax.ShapeDtypeStruct(parts.shape, parts.dtype),
        ],
        scratch_shapes=[
            pltpu.VMEM((group - 1,) + parts.shape[1:], F32),
            pltpu.VMEM(parts.shape[1:], F32),
        ]
        + [sems] * 6,
        compiler_params=pltpu.CompilerParams(
            collective_id=0, has_side_effects=True, vmem_limit_bytes=32 * 1024 * 1024
        ),
        name="return_and_sum",
    )(pieces, parts)
    return field.reshape(grads.shape), total.reshape(acc.shape)


def spread_kernel(group, pieces_ref, arrived_ref, send, recv):
    me = lax.axis_index("gx")
    mine = lax.rem(me, group)
    base = me - mine
    others = [lax.rem(mine + r, group) for r in range(1, group)]
    barrier = pltpu.get_barrier_semaphore()
    for other in others:
        pl.semaphore_signal(
            barrier, inc=1, device_id={"gx": base + other}, device_id_type=pl.DeviceIdType.MESH
        )
    pl.semaphore_wait(barrier, group - 1)
    copies = []
    for at, other in enumerate(others):
        copy = pltpu.make_async_remote_copy(
            src_ref=pieces_ref.at[other],
            dst_ref=arrived_ref.at[mine],
            send_sem=send.at[at],
            recv_sem=recv.at[at],
            device_id={"gx": base + other},
            device_id_type=pl.DeviceIdType.MESH,
        )
        copy.start()
        copies.append(copy)
    arrived_ref[mine] = pieces_ref[mine]
    for copy in copies:
        copy.wait_recv()
    for copy in copies:
        copy.wait_send()


def spread(pieces, group):
    flat = pieces.reshape(group, -1, pieces.shape[-1])
    whole = pl.BlockSpec(memory_space=pltpu.VMEM)
    arrived = pl.pallas_call(
        lambda *refs: spread_kernel(group, *refs),
        in_specs=[whole],
        out_specs=whole,
        out_shape=jax.ShapeDtypeStruct(flat.shape, flat.dtype),
        scratch_shapes=[pltpu.SemaphoreType.DMA((group - 1,))] * 2,
        compiler_params=pltpu.CompilerParams(
            collective_id=1, has_side_effects=True, vmem_limit_bytes=32 * 1024 * 1024
        ),
        name="spread",
    )(flat)
    return arrived.reshape(pieces.shape)


def shift_rows(field, offset, sign):
    count = lax.axis_size("gx")
    for bit_pos in range(3):
        by = sign * (1 << bit_pos)
        moved = lax.ppermute(field, "gx", [(i, (i + by) % count) for i in range(count)])
        field = jnp.where(offset >> bit_pos & 1 == 1, moved, field)
    return field


def per_device(tokens, cotangent, offsets, norm_gain, qkv_weight, proj_weight):
    _, extent_y, extent_z, features = tokens.shape
    count = lax.axis_size("gx")
    group = extent_z // W
    offset_x = offsets[0]
    stacked = jnp.concatenate([tokens, cotangent], 0)
    if count != group:
        stacked = shift_rows(stacked, offset_x, -1)
        offsets = offsets * jnp.array([0, 1, 1], offsets.dtype)
    stacked = jnp.roll(stacked, -offsets[2], axis=2)
    pieces = stacked.reshape(2, extent_y, group, W, features).transpose(2, 0, 1, 3, 4)
    data = spread(pieces, group)
    grads, acc = windows_back(offsets, data, norm_gain, qkv_weight, proj_weight)
    back, total = return_and_sum(grads, acc, group)
    field = back.transpose(1, 0, 2, 3).reshape(1, extent_y, extent_z, features)
    field = jnp.roll(field, offsets[2], axis=2)
    if count != group:
        field = shift_rows(field, offset_x, 1)
        total = lax.psum(total * (1.0 / group), "gx")
    total = total * (count * extent_y * extent_z) ** (-0.5)
    return (
        field,
        total[:, : 3 * features],
        total[:, 3 * features : 4 * features],
        total[0, 4 * features :],
    )


def solution(mesh):
    rows = P(("rve", "gx"), None, None, None)
    return jax.shard_map(
        per_device,
        mesh=mesh,
        in_specs=(rows, rows, P(), P(), P(), P()),
        out_specs=(rows, P("rve", None), P("rve", None), P("rve")),
        check_vma=False,
    )
```
